128 devices in a mesh: blk: 16 (over x_lo, z, core), feat: 8 (over y, x_hi).
Axes of the slice: x: 4 (x_hi: 2, x_lo: 2; x = x_hi * 2 + x_lo), y: 4, z: 4, core: 2. Of those that a mesh axis runs over, the one named last changes fastest.
Arguments:
- node_feats: bfloat16 [65536, 1024], P(('blk', 'feat')), may hold values from -6 to 6
- weight: bfloat16 [1024, 1024], replicated, may hold values from -0.1875 to 0.1875
- bias_vec: float32 [1024], P('feat'), may hold values from -3 to 3
- block_vals: bfloat16 [512, 14, 128, 128], P('blk'), may hold values from -0.1875 to 0.1875
- block_cols: int32 [512, 14], P('blk'), may hold values from 0 to 511, as said below
- row_counts: int32 [512], P('blk'), may hold values from 2 to 14, as said below
- cotangent: bfloat16 [65536, 1024], P('blk', 'feat'), may hold values from -6 to 6
Outputs:
- hidden_out: bfloat16 [65536, 1024], P('blk', 'feat')
- grad_nodes: bfloat16 [65536, 1024], P(('blk', 'feat'))
- grad_weight: float32 [1024, 1024], P('blk', 'feat')
- grad_bias: float32 [1024], P('feat')
The draws below stay inside these ranges and needn't reach their ends.
Inputs may be any that keep to these rules, and one draw needn't show every extreme that they name: `block_cols`: each block row names 14 different block columns. Groups are runs of 512 / 16 consecutive block rows; over all slots of one group's block rows, at most 22 different block columns belong to any one owning group (the group whose nodes they are), and this bound is reached. Only the first row_counts[r] slots of block row r are adjacency blocks; the other slots are ignored.
All inputs are finite; a program needn't handle non-finite values.
Results may differ from the reference program's by a relative error of at most 0.03.
The reference program's roundings to bfloat16 on the way (of `transformed`, `grad_pre` and `grad_mid`) count: a program that leaves them out, or rounds other values in their place, can miss the bound.
Values may be sent and summed in bfloat16 or wider, within the bound.
A program may use at most 192 MiB of HBM per device.

```python
import jax
import jax.numpy as jnp
from jax import lax

FEAT = 1024
BS = 128
KMAX = 14
NODES = 65536
NBLK = 512
N_BLK = 16


def draw_block_cols(key, part):
    key = jax.random.fold_in(key, 11)
    per_group = NBLK // N_BLK
    used_count = max(1, per_group * 11 // 16)
    union_size = used_count * N_BLK
    set_key, order_key, start_key = jax.random.split(key, 3)
    pair_keys = jax.random.split(set_key, N_BLK * N_BLK)
    chosen = jax.vmap(lambda pair_key: jax.random.permutation(pair_key, per_group)[:used_count])(pair_keys).astype(jnp.int32)
    chosen = chosen.reshape(N_BLK, N_BLK, used_count)
    owners = jnp.arange(N_BLK, dtype=jnp.int32)[None, :, None] * per_group
    union_cols = (chosen + owners).reshape(N_BLK, union_size).astype(jnp.int32)
    order_keys = jax.random.split(order_key, N_BLK)
    orders = jax.vmap(lambda order_one: jax.random.permutation(order_one, union_size))(order_keys).astype(jnp.int32)
    starts = jax.random.randint(start_key, (N_BLK,), 0, union_size).astype(jnp.int32)
    row_ids = jnp.arange(per_group, dtype=jnp.int32)[:, None]
    slot_ids = jnp.arange(KMAX, dtype=jnp.int32)[None, :]
    positions = (row_ids * KMAX + slot_ids)[None, :, :] + starts[:, None, None]
    positions = (positions % union_size).astype(jnp.int32)
    picked_pos = jnp.take_along_axis(orders, positions.reshape(N_BLK, -1), axis=1)
    result = jnp.take_along_axis(union_cols, picked_pos, axis=1)
    return result.reshape(NBLK, KMAX).astype(jnp.int32)


def draw_row_counts(key, part):
    key = jax.random.fold_in(key, 12)
    first_key, second_key, third_key = jax.random.split(key, 3)
    counts = jax.random.randint(first_key, (NBLK,), 2, KMAX + 1).astype(jnp.int32)
    full_row = jax.random.randint(second_key, (), 0, NBLK).astype(jnp.int32)
    thin_row = (full_row + 1 + jax.random.randint(third_key, (), 0, NBLK - 1).astype(jnp.int32)) % NBLK
    counts = counts.at[full_row].set(KMAX)
    counts = counts.at[thin_row].set(2)
    return counts.astype(jnp.int32)


def block_levels(stream_key, shape, cuts, low, high):
    loudness = 1.0
    for position, blocks in cuts:
        heights = jax.random.uniform(jax.random.fold_in(jax.random.fold_in(stream_key, 6), position), (blocks,), jnp.float32, low / len(cuts), high / len(cuts))
        loudness = loudness * jnp.repeat(jnp.exp(heights), shape[position] // blocks).reshape((-1,) + (1,) * (len(shape) - 1 - position))
    return loudness


def noise(key, dims, deviation, bound, pieces=(), kind=jnp.bfloat16):
    gain = block_levels(key, dims, pieces, -0.22, 0.18) if pieces else 1.0
    entries = jax.random.normal(key, dims, jnp.float32) * deviation * gain
    return jnp.minimum(jnp.maximum(entries, -bound), bound).astype(kind)


def setup_inputs(seed: int = 0) -> dict:
    key_list = jax.random.split(jax.random.key(seed), 8)
    node_feats = noise(key_list[0], (NODES, FEAT), 1.0, 6.0, ((0, 128),))
    weight = noise(key_list[1], (FEAT, FEAT), FEAT ** -0.5, 0.1875)
    bias_vec = noise(key_list[2], (FEAT,), 0.5, 3.0, ((0, 8),), jnp.float32)
    block_vals = noise(key_list[3], (NBLK, KMAX, BS, BS), (BS * 8) ** -0.5, 0.1875, ((0, 16),))
    block_cols = draw_block_cols(jax.random.fold_in(key_list[7], 71), 0)
    row_counts = draw_row_counts(jax.random.fold_in(key_list[7], 71), 0)
    cotangent = noise(key_list[6], (NODES, FEAT), 1.0, 6.0, ((0, 16), (1, 8)))
    return dict(node_feats=node_feats, weight=weight, bias_vec=bias_vec, block_vals=block_vals, block_cols=block_cols, row_counts=row_counts, cotangent=cotangent)


def reference(node_feats, weight, bias_vec, block_vals, block_cols, row_counts, cotangent):
    transformed = jnp.dot(node_feats, weight, preferred_element_type=jnp.float32).astype(jnp.bfloat16)
    blocks_all = transformed.reshape(NBLK, BS, FEAT)
    slots = jnp.arange(KMAX, dtype=jnp.int32)
    live = slots[None, :] < row_counts[:, None]
    per_group = NBLK // N_BLK
    vals_group = block_vals.reshape(N_BLK, per_group, KMAX, BS, BS)
    cols_group = block_cols.reshape(N_BLK, per_group, KMAX)
    live_group = live.reshape(N_BLK, per_group, KMAX)

    def forward_group(packed):
        values, columns, alive = packed
        picked = blocks_all[columns] * alive[:, :, None, None].astype(jnp.bfloat16)
        return jnp.einsum("rkij,rkjc->ric", values.astype(jnp.float32), picked.astype(jnp.float32))

    summed = lax.map(forward_group, (vals_group, cols_group, live_group)).reshape(NODES, FEAT)
    pre_act = summed + bias_vec[None, :]
    hidden_out = jnp.maximum(pre_act, 0.0).astype(jnp.bfloat16)
    grad_pre = jnp.where(pre_act > 0.0, cotangent.astype(jnp.float32), 0.0).astype(jnp.bfloat16)
    grad_group = grad_pre.reshape(N_BLK, per_group, BS, FEAT)

    def backward_group(total, packed):
        values, columns, alive, grads = packed
        contrib = jnp.einsum("rkij,ric->rkjc", values.astype(jnp.float32), grads.astype(jnp.float32))
        contrib = contrib * alive[:, :, None, None].astype(jnp.float32)
        term = jax.ops.segment_sum(contrib.reshape(-1, BS, FEAT), columns.reshape(-1), num_segments=NBLK)
        term = lax.optimization_barrier(term.astype(jnp.bfloat16))
        return total + term.astype(jnp.float32), None

    start_total = jnp.zeros((NBLK, BS, FEAT), jnp.float32)
    total, _ = lax.scan(backward_group, start_total, (vals_group, cols_group, live_group, grad_group))
    grad_mid = total.reshape(NODES, FEAT).astype(jnp.bfloat16)
    grad_nodes = jnp.dot(grad_mid, weight.T, preferred_element_type=jnp.float32).astype(jnp.bfloat16)
    grad_weight = lax.dot_general(node_feats, grad_mid, (((0,), (0,)), ((), ())), preferred_element_type=jnp.float32)
    grad_bias = jnp.sum(grad_pre.astype(jnp.float32), axis=0)
    return hidden_out, grad_nodes, grad_weight, grad_bias
```

```python
import jax
import jax.numpy as jnp
from jax import lax
from jax.experimental import pallas as pl
from jax.experimental.pallas import tpu as pltpu
from jax.sharding import PartitionSpec as P

MESH = pl.DeviceIdType.MESH
BF = jnp.bfloat16
F32 = jnp.float32
N_FEAT = 8
N_GRP = 16
ROWS = 512
COL = 128
BS = 128
KMAX = 14
PER = 32
VMEM_BYTES = 56 * 2**20
OWN, PX, NP, NM, PA, PB, FC, FD = range(8)


def place():
    b = lax.axis_index("blk")
    f = lax.axis_index("feat")
    xl = lax.div(b, 8)
    z = lax.rem(lax.div(b, 2), 4)
    c = lax.rem(b, 2)
    return xl, z, c, f


def grp(xl, z, c):
    return xl * 8 + z * 2 + c


def zadd(z, d):
    return lax.rem(z + d, 4)


def units(xl, z, c):
    o = 1 - xl
    return (
        grp(xl, z, c),
        grp(o, z, c),
        grp(xl, zadd(z, 1), c),
        grp(xl, zadd(z, 3), c),
        grp(o, zadd(z, 1), c),
        grp(o, zadd(z, 3), c),
        grp(xl, zadd(z, 2), c),
        grp(o, zadd(z, 2), c),
    )


def rcopy(src, dst, ssem, rsem, dev):
    return pltpu.make_async_remote_copy(
        src_ref=src, dst_ref=dst, send_sem=ssem, recv_sem=rsem, device_id=dev, device_id_type=MESH
    )


def greet(peers):
    bar = pltpu.get_barrier_semaphore()
    for dev in peers:
        pl.semaphore_signal(bar, inc=1, device_id=dev, device_id_type=MESH)
    pl.semaphore_wait(bar, len(peers))


def each(lo, hi, body):
    def step(i, carry):
        body(i)
        return carry

    lax.fori_loop(lo, hi, step, 0)


def gather_kernel(x_ref, w_ref, t_ref, tr, a_send, a_recv, o_send, f_send, s_send, recv, s_recv, l_sem):
    xl, z, c, f = place()
    u = units(xl, z, c)
    g = u[OWN]
    dx = {"blk": u[PX], "feat": f}
    dzp = {"blk": u[NP], "feat": f}
    dzm = {"blk": u[NM], "feat": f}
    ds = {"blk": grp(xl, z, 1 - c), "feat": f}
    greet([dx, dzp, dzm, ds] + [{"blk": g, "feat": lax.rem(f + i, N_FEAT)} for i in range(1, N_FEAT)])

    def chunk(i):
        return lax.rem(f + N_FEAT - i, N_FEAT)

    def product(i):
        to = lax.rem(f + i, N_FEAT)
        cols = pl.ds(pl.multiple_of(to * COL, COL), COL)
        tr[i] = jnp.dot(x_ref[...], w_ref[:, cols], preferred_element_type=F32).astype(BF)
        return to

    def a2a(i, to):
        return rcopy(tr.at[i], t_ref.at[g, f], a_send.at[i], a_recv.at[i], {"blk": g, "feat": to})

    def send_first(i):
        to = product(i)
        a2a(i, to).start()

    each(1, N_FEAT, send_first)
    product(0)
    mine = pltpu.make_async_copy(tr.at[0], t_ref.at[g, f], l_sem)
    mine.start()
    mine.wait()

    def own_copy(k, i, dev, r):
        p = t_ref.at[g, chunk(i)]
        return rcopy(p, p, o_send.at[k, i], recv.at[r, i], dev)

    def sib_copy(k, i):
        p = t_ref.at[u[k], chunk(i)]
        return rcopy(p, p, s_send.at[k, i], s_recv.at[k, i], ds)

    def fwd(k, i, slot, dev, r):
        p = t_ref.at[u[k], chunk(i)]
        return rcopy(p, p, f_send.at[slot, lax.rem(i, 4)], recv.at[r, i], dev)

    def arrived(k, i):
        p = t_ref.at[u[k], chunk(i)]
        rcopy(p, p, l_sem, recv.at[k, i], dx).wait_recv()

    def own_all(i):
        own_copy(0, i, dx, PX).start()
        own_copy(1, i, dzp, NM).start()
        own_copy(2, i, dzm, NP).start()
        sib_copy(OWN, i).start()

    own_all(0)

    def own_next(i):
        p = t_ref.at[g, chunk(i)]
        rcopy(p, p, l_sem, a_recv.at[i], dx).wait_recv()
        own_all(i)

    each(1, N_FEAT, own_next)

    def low(i):
        arrived(PX, i)
        fwd(PX, i, 0, dzm, PA).start()
        sib_copy(PX, i).start()
        arrived(NP, i)
        fwd(NP, i, 1, dzm, FC).start()
        sib_copy(NP, i).start()
        arrived(NM, i)
        fwd(NM, i, 2, dx, PB).start()
        sib_copy(NM, i).start()

    def high(i):
        arrived(PX, i)
        fwd(PX, i, 3, dzp, PB).start()
        sib_copy(PX, i).start()
        arrived(NM, i)
        fwd(NM, i, 4, dzp, FC).start()
        sib_copy(NM, i).start()
        arrived(NP, i)
        fwd(NP, i, 5, dx, PA).start()
        sib_copy(NP, i).start()

    each(0, 4, low)
    each(4, 8, high)

    def last(i):
        arrived(PA, i)
        fwd(PA, i, 6, dzm, FD).start()
        sib_copy(PA, i).start()
        arrived(PB, i + 4)
        fwd(PB, i + 4, 7, dzp, FD).start()
        sib_copy(PB, i + 4).start()

    each(0, 4, last)

    def rest(i):
        arrived(PA, i + 4)
        sib_copy(PA, i + 4).start()
        arrived(PB, i)
        sib_copy(PB, i).start()
        arrived(FC, i)
        sib_copy(FC, i).start()
        arrived(FC, i + 4)
        sib_copy(FC, i + 4).start()

    each(0, 4, rest)

    def far(i):
        arrived(FD, i)
        sib_copy(FD, i).start()

    each(0, 8, far)

    def finish(i):
        own_copy(0, i, dx, PX).wait_send()
        own_copy(1, i, dzp, NM).wait_send()
        own_copy(2, i, dzm, NP).wait_send()
        for k in range(8):
            sib_copy(k, i).wait_send()
            p = t_ref.at[u[k], chunk(i)]
            rcopy(p, p, l_sem, s_recv.at[k, i], ds).wait_recv()

    each(0, 8, finish)

    def finish_fwd(i):
        for slot, k in enumerate((PX, NP, NM, PX, NM, NP, PA, PB)):
            p = t_ref.at[u[k], chunk(i)]
            rcopy(p, p, f_send.at[slot, i], recv.at[0, i], dx).wait_send()

    each(0, 4, finish_fwd)

    def finish_a2a(i):
        a2a(i, lax.rem(f + i, N_FEAT)).wait_send()

    each(1, N_FEAT, finish_a2a)


def gather_call(x, w):
    dma = pltpu.SemaphoreType.DMA
    return pl.pallas_call(
        gather_kernel,
        out_shape=jax.ShapeDtypeStruct((N_GRP, N_FEAT, ROWS, COL), BF),
        in_specs=[pl.BlockSpec(memory_space=pltpu.VMEM)] * 2,
        out_specs=pl.BlockSpec(memory_space=pltpu.HBM),
        scratch_shapes=[
            pltpu.VMEM((N_FEAT, ROWS, COL), BF),
            dma((8,)),
            dma((8,)),
            dma((3, 8)),
            dma((8, 4)),
            dma((8, 8)),
            dma((8, 8)),
            dma((8, 8)),
            dma,
        ],
        compiler_params=pltpu.CompilerParams(
            collective_id=0, has_side_effects=True, vmem_limit_bytes=VMEM_BYTES
        ),
        name="gather",
    )(x, w)


def block_kernel(cols, cnt, v_ref, cot_ref, bias_ref, t_ref, hid_ref, q_ref, bsum_ref, tbuf, acc, qbuf, seen, tsem, qsem):
    r = pl.program_id(0)

    def fetch(row, slot, k):
        return pltpu.make_async_copy(t_ref.at[cols[row, k]], tbuf.at[slot, k], tsem.at[slot, k])

    @pl.when(r == 0)
    def _():
        def clear(i):
            seen[i] = 0

        each(0, N_GRP * PER, clear)
        bsum_ref[...] = jnp.zeros_like(bsum_ref)
        for k in range(KMAX):
            fetch(0, 0, k).start()

    slot = lax.rem(r, 2)

    @pl.when(r + 1 < PER)
    def _():
        for k in range(KMAX):
            fetch(r + 1, 1 - slot, k).start()

    for k in range(KMAX):
        fetch(r, slot, k).wait()

    n = cnt[r]

    def pair(p):
        a = jnp.where(2 * p < n, v_ref[0, 2 * p], jnp.zeros((BS, BS), BF))
        b = jnp.where(2 * p + 1 < n, v_ref[0, 2 * p + 1], jnp.zeros((BS, BS), BF))
        return jnp.concatenate([a, b], axis=1)

    pre = jnp.zeros((BS, COL), F32)
    for p in range(KMAX // 2):
        rhs = tbuf[slot, 2 * p : 2 * p + 2].reshape(2 * BS, COL)
        pre = pre + jnp.dot(pair(p), rhs, preferred_element_type=F32)
    pre = pre + bias_ref[...]
    hid_ref[...] = jnp.maximum(pre, 0.0).astype(BF)
    grad = jnp.where(pre > 0.0, cot_ref[...].astype(F32), 0.0)
    bsum_ref[...] += jnp.sum(grad.reshape(BS // 8, 8, COL), axis=0)
    grad_t = grad.T.astype(BF)
    prods = []
    for p in range(KMAX // 2):
        prods.append(jnp.dot(grad_t, pair(p), preferred_element_type=F32))
    for k in range(KMAX):
        col = cols[r, k]
        live = k < n
        old = seen[col]
        seen[col] = jnp.where(live, 1, old)
        part = prods[k // 2][:, (k % 2) * BS : (k % 2 + 1) * BS]

        @pl.when(live & (old == 0))
        def _():
            acc[col] = part

        @pl.when(live & (old != 0))
        def _():
            acc[col] += part

    @pl.when(r == PER - 1)
    def _():
        def out_copy(i):
            return pltpu.make_async_copy(qbuf.at[lax.rem(i, 2)], q_ref.at[i], qsem.at[lax.rem(i, 2)])

        def group(i):
            @pl.when(i >= 2)
            def _():
                out_copy(i - 2).wait()

            def block(j):
                b = i * PER + j
                qbuf[lax.rem(i, 2), j] = jnp.where(seen[b] != 0, acc[b], 0.0).astype(BF)

            each(0, PER, block)
            out_copy(i).start()

        each(0, N_GRP, group)
        out_copy(N_GRP - 2).wait()
        out_copy(N_GRP - 1).wait()


def block_call(cols, cnt, vals, cot, bias, t):
    rows = PER * BS
    return pl.pallas_call(
        block_kernel,
        out_shape=(
            jax.ShapeDtypeStruct((rows, COL), BF),
            jax.ShapeDtypeStruct((N_GRP, PER, BS, BS), BF),
            jax.ShapeDtypeStruct((8, COL), F32),
        ),
        grid_spec=pltpu.PrefetchScalarGridSpec(
            num_scalar_prefetch=2,
            grid=(PER,),
            in_specs=[
                pl.BlockSpec((1, KMAX, BS, BS), lambda r, *_: (r, 0, 0, 0)),
                pl.BlockSpec((BS, COL), lambda r, *_: (r, 0)),
                pl.BlockSpec((1, COL), lambda r, *_: (0, 0)),
                pl.BlockSpec(memory_space=pltpu.HBM),
            ],
            out_specs=[
                pl.BlockSpec((BS, COL), lambda r, *_: (r, 0)),
                pl.BlockSpec(memory_space=pltpu.HBM),
                pl.BlockSpec((8, COL), lambda r, *_: (0, 0)),
            ],
            scratch_shapes=[
                pltpu.VMEM((2, KMAX, BS, COL), BF),
                pltpu.VMEM((N_GRP * PER, BS, BS), F32),
                pltpu.VMEM((2, PER, BS, BS), BF),
                pltpu.SMEM((N_GRP * PER,), jnp.int32),
                pltpu.SemaphoreType.DMA((2, KMAX)),
                pltpu.SemaphoreType.DMA((2,)),
            ],
        ),
        compiler_params=pltpu.CompilerParams(vmem_limit_bytes=VMEM_BYTES),
        name="blocks",
    )(cols, cnt, vals, cot, bias, t)


def scatter_kernel(
    q_ref, bsum_ref, x_ref, w_ref, gn_ref, gw_ref, gb_ref,
    own, sib, zp, zm, xp, zp_o, zm_o, x_o, gmo, gm, xt, gwp, gwsib, gws, gwr, gw2, gw2r, bsib, bpl,
    own_sem, sib_send, sib_recv, d_send, d_recv, o_send, o_recv, m_send, m_recv,
    ws_send, ws_recv, wf_send, wf_recv, wp_send, wp_recv, b_send, b_recv, l_sem,
):
    xl, z, c, f = place()
    u = units(xl, z, c)
    v = units(xl, z, 1 - c)
    g = u[OWN]
    q = xl * 4 + z
    dx = {"blk": u[PX], "feat": f}
    dzp = {"blk": u[NP], "feat": f}
    dzm = {"blk": u[NM], "feat": f}
    ds = {"blk": v[OWN], "feat": f}

    def feat_dev(i):
        return {"blk": g, "feat": lax.rem(f + i, N_FEAT)}

    def plane_dev(i):
        return {"blk": lax.rem(q + i, 8) * 2 + c, "feat": f}

    greet([ds] + [feat_dev(i) for i in range(1, 8)] + [plane_dev(i) for i in range(1, 8)])

    bs_copy = rcopy(bsum_ref, bsib, b_send.at[0], b_recv.at[0], ds)
    bs_copy.start()

    order = (FD, PA, PB, FC, PX, NP, NM, OWN)

    def mine_copy(k):
        return pltpu.make_async_copy(q_ref.at[u[k]], own.at[k], own_sem.at[k])

    def sib_copy(k):
        return rcopy(q_ref.at[v[k]], sib.at[k], sib_send.at[k], sib_recv.at[k], ds)

    def begin(k):
        mine_copy(k).start()
        sib_copy(k).start()

    def have(k):
        mine_copy(k).wait()
        sib_copy(k).wait()

    def chunk(i):
        return lax.rem(f + N_FEAT - 1 - i, N_FEAT)

    def total(k, i, *more):
        ch = chunk(i)
        s = own[k, ch].astype(F32) + sib[k, ch].astype(F32)
        for m in more:
            s = s + m.astype(F32)
        return s

    def ship(slot, j, k, i, dst, dev):
        return rcopy(own.at[k, chunk(i)], dst, d_send.at[slot, j], d_recv.at[slot, j], dev)

    def ship_o(slot, k, i, dst, dev):
        return rcopy(own.at[k, chunk(i)], dst, o_send.at[slot, i], o_recv.at[slot, i], dev)

    def put(k, i, value):
        own[k, chunk(i)] = value.astype(BF)

    def got(slot, j):
        ship(slot, j, 0, 0, zp.at[0, j], dx).wait_recv()

    begin(FD)
    begin(PA)
    have(FD)
    begin(PB)

    def send_d(j):
        put(FD, j, total(FD, j))
        ship(0, j, FD, j, zp.at[0, j], dzp).start()
        put(FD, j + 4, total(FD, j + 4))
        ship(1, j, FD, j + 4, zm.at[0, j], dzm).start()

    each(0, 4, send_d)
    have(PA)
    begin(FC)

    def send_a(j):
        put(PA, j + 4, total(PA, j + 4))
        ship(2, j, PA, j + 4, xp.at[0, j], dx).start()

    each(0, 4, send_a)
    have(PB)
    begin(PX)

    def send_b(j):
        put(PB, j, total(PB, j))
        ship(3, j, PB, j, xp.at[1, j], dx).start()

    each(0, 4, send_b)
    have(FC)
    begin(NP)

    def send_c(j):
        put(FC, j, total(FC, j))
        ship(4, j, FC, j, zp.at[2, j], dzp).start()
        put(FC, j + 4, total(FC, j + 4))
        ship(5, j, FC, j + 4, zm.at[2, j], dzm).start()

    each(0, 4, send_c)
    have(PX)
    begin(NM)

    def send_ab(j):
        got(0, j)
        put(PA, j, total(PA, j, zp[0, j]))
        ship(6, j, PA, j, zp.at[1, j], dzp).start()
        got(1, j)
        put(PB, j + 4, total(PB, j + 4, zm[0, j]))
        ship(7, j, PB, j + 4, zm.at[1, j], dzm).start()

    each(0, 4, send_ab)
    have(NP)
    begin(OWN)
    have(NM)

    for a in range(8):
        for b in range(4):
            xt[a * 128 : (a + 1) * 128, b * 128 : (b + 1) * 128] = (
                x_ref[b * 128 : (b + 1) * 128, a * 128 : (a + 1) * 128].astype(F32).T.astype(BF)
            )
    bs_copy.wait()
    bpl[q] = bsum_ref[...] + bsib[...]

    def b_copy(i):
        return rcopy(bpl.at[q], bpl.at[q], b_send.at[i], b_recv.at[i], plane_dev(i))

    each(1, 8, lambda i: b_copy(i).start())

    def send_n_low(j):
        got(4, j)
        put(NP, j, total(NP, j, zp[2, j]))
        ship_o(0, NP, j, zp_o.at[j], dzp).start()
        got(3, j)
        put(NM, j, total(NM, j, xp[1, j]))
        ship_o(1, NM, j, zm_o.at[j], dzm).start()

    each(0, 4, send_n_low)

    def send_p(j):
        got(6, j)
        put(PX, j, total(PX, j, zp[1, j]))
        ship_o(2, PX, j, x_o.at[j], dx).start()

    each(0, 4, send_p)

    def send_n_high(j):
        i = j + 4
        got(2, j)
        put(NP, i, total(NP, i, xp[0, j]))
        ship_o(0, NP, i, zp_o.at[i], dzp).start()
        got(5, j)
        put(NM, i, total(NM, i, zm[2, j]))
        ship_o(1, NM, i, zm_o.at[i], dzm).start()
        got(7, j)
        put(PX, i, total(PX, i, zm[1, j]))
        ship_o(2, PX, i, x_o.at[i], dx).start()

    each(0, 4, send_n_high)
    have(OWN)

    def m_copy(i):
        cols = pl.ds(pl.multiple_of(f * COL, COL), COL)
        return rcopy(gmo.at[i], gm.at[:, cols], m_send.at[i], m_recv.at[i], {"blk": g, "feat": chunk(i)})

    def own_part(i):
        for slot, dst in enumerate((zp_o, zm_o, x_o)):
            rcopy(own.at[NP, 0], dst.at[i], l_sem, o_recv.at[slot, i], dx).wait_recv()
        s = total(OWN, i, zp_o[i], zm_o[i], x_o[i])
        for b in range(4):
            gmo[i, b * BS : (b + 1) * BS, :] = s[b * BS : (b + 1) * BS].T.astype(BF)

    def own_send(i):
        own_part(i)
        m_copy(i).start()

    each(0, 7, own_send)
    own_part(7)
    here = pltpu.make_async_copy(gmo.at[7], gm.at[:, pl.ds(pl.multiple_of(f * COL, COL), COL)], l_sem)
    here.start()
    here.wait()
    each(0, 7, lambda i: m_copy(i).wait())

    for j in range(4):
        part = jnp.dot(xt[...], gm[:, j * 256 : (j + 1) * 256], preferred_element_type=F32).astype(BF)
        gwp[2 * j] = part[:, :128].reshape(8, 2, 64, 128)
        gwp[2 * j + 1] = part[:, 128:].reshape(8, 2, 64, 128)
    ws = rcopy(gwp.at[:, :, 1 - c], gwsib, ws_send, ws_recv, ds)
    ws.start()
    for j in range(2):
        gn_ref[:, j * 256 : (j + 1) * 256] = lax.dot_general(
            gm[...], w_ref[j * 256 : (j + 1) * 256, :], (((1,), (1,)), ((), ())), preferred_element_type=F32
        ).astype(BF)
    ws.wait()

    def wf_copy(i):
        return rcopy(gws.at[lax.rem(f + i, N_FEAT)], gwr.at[i], wf_send.at[i], wf_recv.at[i], feat_dev(i))

    def wf_sum(i):
        to = lax.rem(f + i, N_FEAT)
        gws[to] = (gwp[to, :, c].astype(F32) + gwsib[to].astype(F32)).astype(BF)

    def wf_step(i):
        wf_sum(i)
        wf_copy(i).start()

    each(1, 8, wf_step)
    wf_sum(0)
    for j in range(2, 4):
        gn_ref[:, j * 256 : (j + 1) * 256] = lax.dot_general(
            gm[...], w_ref[j * 256 : (j + 1) * 256, :], (((1,), (1,)), ((), ())), preferred_element_type=F32
        ).astype(BF)
    each(1, 8, lambda i: b_copy(i).wait())
    gb_ref[...] = jnp.sum(jnp.sum(bpl[...], axis=0), axis=0, keepdims=True)
    each(1, 8, lambda i: wf_copy(i).wait())

    def wp_copy(i):
        return rcopy(gw2.at[lax.rem(q + i, 8)], gw2r.at[i], wp_send.at[i], wp_recv.at[i], plane_dev(i))

    def wp_sum(i):
        to = lax.rem(q + i, 8)
        s = gws[f, to].astype(F32)
        for k in range(1, 8):
            s = s + gwr[k, to].astype(F32)
        return to, s

    def wp_step(i):
        to, s = wp_sum(i)
        gw2[to] = s.astype(BF)
        wp_copy(i).start()

    each(1, 8, wp_step)
    s = wp_sum(0)[1]
    each(1, 8, lambda i: wp_copy(i).wait())
    for k in range(1, 8):
        s = s + gw2r[k].astype(F32)
    gw_ref[...] = s

    def finish(j):
        for slot in range(8):
            ship(slot, j, 0, 0, zp.at[0, j], dx).wait_send()

    each(0, 4, finish)

    def finish_o(i):
        for slot, dst in enumerate((zp_o, zm_o, x_o)):
            ship_o(slot, NP, i, dst.at[i], dx).wait_send()

    each(0, 8, finish_o)


def scatter_call(q, bsum, x, w):
    dma = pltpu.SemaphoreType.DMA
    unit = (8, ROWS, COL)
    vm = pltpu.VMEM
    spec = pl.BlockSpec(memory_space=pltpu.VMEM)
    return pl.pallas_call(
        scatter_kernel,
        out_shape=(
            jax.ShapeDtypeStruct((ROWS, N_FEAT * COL), BF),
            jax.ShapeDtypeStruct((64, COL), F32),
            jax.ShapeDtypeStruct((1, COL), F32),
        ),
        in_specs=[pl.BlockSpec(memory_space=pltpu.HBM), spec, spec, spec],
        out_specs=(spec, spec, spec),
        scratch_shapes=[
            vm((8,) + unit, BF),
            vm((8,) + unit, BF),
            vm((3, 4, ROWS, COL), BF),
            vm((3, 4, ROWS, COL), BF),
            vm((2, 4, ROWS, COL), BF),
            vm(unit, BF),
            vm(unit, BF),
            vm(unit, BF),
            vm(unit, BF),
            vm((ROWS, N_FEAT * COL), BF),
            vm((N_FEAT * COL, ROWS), BF),
            vm((8, 8, 2, 64, 128), BF),
            vm((8, 8, 64, 128), BF),
            vm((8, 8, 64, 128), BF),
            vm((8, 8, 64, 128), BF),
            vm((8, 64, 128), BF),
            vm((8, 64, 128), BF),
            vm((8, COL), F32),
            vm((8, 8, COL), F32),
            dma((8,)),
            dma((8,)),
            dma((8,)),
            dma((8, 4)),
            dma((8, 4)),
            dma((3, 8)),
            dma((3, 8)),
            dma((8,)),
            dma((8,)),
            dma,
            dma,
            dma((8,)),
            dma((8,)),
            dma((8,)),
            dma((8,)),
            dma((8,)),
            dma((8,)),
            dma,
        ],
        compiler_params=pltpu.CompilerParams(
            collective_id=1, has_side_effects=True, vmem_limit_bytes=VMEM_BYTES
        ),
        name="scatter",
    )(q, bsum, x, w)


def local(node_feats, weight, bias_vec, block_vals, block_cols, row_counts, cotangent):
    t = gather_call(node_feats, weight).reshape(N_GRP * PER, BS, COL)
    hidden, q, bsum = block_call(
        block_cols, row_counts, block_vals, cotangent, bias_vec.reshape(1, COL), t
    )
    gn, gw, gb = scatter_call(q.reshape(N_GRP, N_FEAT, ROWS, COL), bsum, node_feats, weight)
    return hidden, gn, gw, gb.reshape(COL)


def solution(mesh):
    in_specs = (
        P(("blk", "feat"), None),
        P(),
        P("feat"),
        P("blk", None, None, None),
        P("blk", None),
        P("blk"),
        P("blk", "feat"),
    )
    out_specs = (P("blk", "feat"), P(("blk", "feat"), None), P("blk", "feat"), P("feat"))
    return jax.shard_map(local, mesh=mesh, in_specs=in_specs, out_specs=out_specs, check_vma=False)
```
